512 devices in a mesh: seq: 64 (over z, y), head: 8 (over x, core).
Axes of the slice: x: 4, y: 8, z: 8, core: 2. Of those that a mesh axis runs over, the one named last changes fastest.
Arguments:
- queries: bfloat16 [24576, 5120], P(('seq', 'head')), may hold values from -30 to 30
- keys: bfloat16 [24576, 5120], P(('seq', 'head')), may hold values from -30 to 30
- values: bfloat16 [24576, 5120], P(('seq', 'head')), may hold values from -6 to 6
- routes: int32 [192, 3], replicated, may hold values from 0 to 191, as said below
- shot_pairs: int32 [24, 2], replicated, may hold values from 0 to 7, as said below
Outputs:
- attention: bfloat16 [24576, 5120], P(('seq', 'head'))
The draws below stay inside these ranges and needn't reach their ends.
Inputs may be any that keep to these rules, and one draw needn't show every extreme that they name: `routes`: each query group's list names 3 distinct groups, all held by indices of seq of other shots at the same place within their shot; the query groups of one block name at most 3 groups of any one other block. `shot_pairs`: each row names two different shots.
All inputs are finite; a program needn't handle non-finite values.
Results may differ from the reference program's by a relative error of at most 0.0046.
Values may be sent and summed in bfloat16 or wider, within the bound.
No kernel may reach another device: no remote copies, remote signals or barrier semaphores. Data moves between devices by JAX's collectives and lax.ppermute only.
A program may use at most 64 MiB of HBM per device.

```python
import jax
import jax.numpy as jnp
from jax import lax

HEADS = 40
HD = 128
TOK_SEQ = 384
GROUP = 128
SHOT_DEV = 8
ROUTED = 3
CAP = 3
TOKENS = 24576
GROUPS = 192
SHOTS = 8
PAIRS = 24


def route_table(key):
    key = jax.random.fold_in(key, 21)
    blocks = TOKENS // TOK_SEQ
    per_block = TOK_SEQ // GROUP
    shots = blocks // SHOT_DEV

    def one_block(block_key, block_index):
        order_key, pick_key = jax.random.split(block_key)
        my_shot = block_index // SHOT_DEV
        position = block_index % SHOT_DEV
        offsets = 1 + jax.random.permutation(order_key, shots - 1)
        sources = (my_shot + offsets) % shots * SHOT_DEV + position
        picks = jax.vmap(lambda pick: jax.random.permutation(pick, per_block)[:CAP])(jax.random.split(pick_key, shots - 1))
        listing = (sources[:, None] * per_block + picks).reshape(-1)
        length = listing.shape[0]
        places = (jnp.arange(per_block, dtype=jnp.int32)[:, None] * ROUTED + jnp.arange(ROUTED, dtype=jnp.int32)[None, :]) % length
        return listing[places]
    result = jax.vmap(one_block)(jax.random.split(key, blocks), jnp.arange(blocks, dtype=jnp.int32))
    return result.reshape(GROUPS, ROUTED).astype(jnp.int32)


def pair_list(key):
    key = jax.random.fold_in(key, 22)
    first_key, second_key = jax.random.split(key)
    first = jax.random.randint(first_key, (PAIRS,), 0, SHOTS, dtype=jnp.int32)
    second = (first + jax.random.randint(second_key, (PAIRS,), 1, SHOTS, dtype=jnp.int32)) % SHOTS
    return jnp.stack((first, second), axis=1).astype(jnp.int32)


def draw_queries(key, part):
    key = jax.random.fold_in(key, 11)
    fresh = jnp.clip(jax.random.normal(key, (TOKENS, HEADS * HD), jnp.float32), -4.0, 4.0)
    return fresh.astype(jnp.bfloat16)


def draw_keys(key, part):
    key = jax.random.fold_in(key, 12)
    fresh = jnp.clip(jax.random.normal(key, (TOKENS, HEADS * HD), jnp.float32), -4.0, 4.0)
    return fresh.astype(jnp.bfloat16)


def draw_routes(key, part):
    return route_table(key)


def draw_shot_pairs(key, part):
    return pair_list(key)


def steps_of(own_key, shape, cuts, least, high):
    loudness = 1.0
    for dim, shards_of in cuts:
        draws = jax.random.uniform(jax.random.fold_in(jax.random.fold_in(own_key, 6), dim), (shards_of,), jnp.float32, least / len(cuts), high / len(cuts))
        loudness = loudness * jnp.repeat(jnp.exp(draws), shape[dim] // shards_of).reshape((-1,) + (1,) * (len(shape) - 1 - dim))
    return loudness


def noise(own_key, shape, spread, bound, shards=(), kind=jnp.bfloat16):
    entries = jax.random.normal(own_key, shape, jnp.float32) * spread
    if len(shards) > 0:
        entries = steps_of(own_key, shape, shards, -0.22, 0.18) * entries
    return jnp.clip(entries, min=-bound, max=bound).astype(kind)


def setup_inputs(seed: int = 0) -> dict:
    arg_keys = jax.random.split(jax.random.key(seed), 6)
    queries = draw_queries(jax.random.fold_in(arg_keys[5], 71), 0)
    keys = draw_keys(jax.random.fold_in(arg_keys[5], 71), 0)
    values = noise(arg_keys[2], (TOKENS, HEADS * HD), 1.0, 6.0, ((0, 512),))
    routes = draw_routes(jax.random.fold_in(arg_keys[5], 71), 0)
    shot_pairs = draw_shot_pairs(jax.random.fold_in(arg_keys[5], 71), 0)
    return {"queries": queries, "keys": keys, "values": values, "routes": routes, "shot_pairs": shot_pairs}


def pair_table(shot_pairs, shots):
    shot_ids = jnp.arange(shots, dtype=jnp.int32)
    first_match = shot_pairs[:, 0][:, None, None] == shot_ids[None, :, None]
    second_match = shot_pairs[:, 1][:, None, None] == shot_ids[None, None, :]
    linked = jnp.any(first_match & second_match, axis=0)
    return linked | linked.T


def reference(queries, keys, values, routes, shot_pairs):
    blocks = TOKENS // TOK_SEQ
    per_block = TOK_SEQ // GROUP
    shots = blocks // SHOT_DEV
    linked = pair_table(shot_pairs, shots)
    score_scale = 1.0 / (HD ** 0.5)
    key_groups = keys.reshape(GROUPS, GROUP, HEADS, HD)
    value_groups = values.reshape(GROUPS, GROUP, HEADS, HD)

    def one_block(inputs):
        query_block, key_block, value_block, route_block, block_index = inputs
        my_shot = block_index // SHOT_DEV
        flat_routes = route_block.reshape(-1).astype(jnp.int32)
        route_shots = flat_routes // per_block // SHOT_DEV
        allowed = linked[my_shot, route_shots].reshape(per_block, ROUTED)
        reachable = jnp.repeat(allowed, GROUP, axis=1)
        query_heads = query_block.reshape(TOK_SEQ, HEADS, HD).astype(jnp.float32)
        local_keys = key_block.reshape(TOK_SEQ, HEADS, HD).astype(jnp.float32)
        local_values = value_block.reshape(TOK_SEQ, HEADS, HD).astype(jnp.float32)
        far_keys = jnp.take(key_groups, flat_routes, axis=0).reshape(per_block, ROUTED * GROUP, HEADS, HD).astype(jnp.float32)
        far_values = jnp.take(value_groups, flat_routes, axis=0).reshape(per_block, ROUTED * GROUP, HEADS, HD).astype(jnp.float32)
        local_scores = jnp.einsum("thd,shd->hts", query_heads, local_keys) * score_scale
        query_groups = query_heads.reshape(per_block, GROUP, HEADS, HD)
        far_scores = jnp.einsum("cqhd,ckhd->hcqk", query_groups, far_keys) * score_scale
        far_scores = jnp.where(reachable[None, :, None, :], far_scores, jnp.float32(-1e30))
        row_max = jnp.maximum(jnp.max(local_scores, axis=-1), jnp.max(far_scores, axis=-1).reshape(HEADS, TOK_SEQ))
        local_weights = jnp.exp(local_scores - row_max[:, :, None])
        far_weights = jnp.exp(far_scores - row_max.reshape(HEADS, per_block, GROUP)[..., None])
        totals = jnp.sum(local_weights, axis=-1) + jnp.sum(far_weights, axis=-1).reshape(HEADS, TOK_SEQ)
        local_rounded = lax.optimization_barrier(local_weights.astype(jnp.bfloat16)).astype(jnp.float32)
        far_rounded = lax.optimization_barrier(far_weights.astype(jnp.bfloat16)).astype(jnp.float32)
        numerator = jnp.einsum("hts,shd->thd", local_rounded, local_values)
        numerator = numerator + jnp.einsum("hcqk,ckhd->cqhd", far_rounded, far_values).reshape(TOK_SEQ, HEADS, HD)
        result = numerator / totals.T[:, :, None]
        return result.reshape(TOK_SEQ, HEADS * HD).astype(jnp.bfloat16)

    inputs = (queries.reshape(blocks, TOK_SEQ, HEADS * HD), keys.reshape(blocks, TOK_SEQ, HEADS * HD),
              values.reshape(blocks, TOK_SEQ, HEADS * HD), routes.reshape(blocks, per_block, ROUTED),
              jnp.arange(blocks, dtype=jnp.int32))
    outcome = lax.map(one_block, inputs)
    return outcome.reshape(TOKENS, HEADS * HD)
```

```python
import functools

import jax
import jax.numpy as jnp
from jax import lax
from jax.experimental import pallas as pl
from jax.experimental.pallas import tpu as pltpu
from jax.sharding import PartitionSpec as P

HD = 128
GROUP = 128
SHOT_DEV = 8
ROUTED = 3
SHOTS = 8
PER_BLOCK = 3
FAR = PER_BLOCK * ROUTED
HALF = GROUP // 2


def hop(value, axis, shots):
    count = lax.axis_size(axis)
    steps = shots * SHOT_DEV
    pairs = [(source, (source + steps) % count) for source in range(count)]
    return lax.ppermute(value, axis, pairs)


def to_heads(rows):
    tokens, features = rows.shape
    parts = lax.axis_size("head")
    pieces = rows.reshape(tokens, parts, features // parts).transpose(1, 0, 2)
    got = lax.all_to_all(pieces, "head", split_axis=0, concat_axis=0, tiled=True)
    return got.reshape(parts * tokens, features // parts)


def to_tokens(block):
    parts = lax.axis_size("head")
    tokens, features = block.shape
    pieces = block.reshape(parts, tokens // parts, features)
    got = lax.all_to_all(pieces, "head", split_axis=0, concat_axis=0, tiled=True)
    return got.transpose(1, 0, 2).reshape(tokens // parts, parts * features)


def ring(block):
    middle = block.shape[0] // 2
    before, after = [block], [block]
    for _ in range(3):
        before.append(hop(before[-1], "seq", 1))
        after.append(hop(after[-1], "seq", -1))
    upper = hop(before[-1][:middle], "seq", 1)
    lower = hop(after[-1][middle:], "seq", -1)
    return (after[1], after[2], after[3], before[3], before[2], before[1], upper, lower)


def pair_table(shot_pairs, shots):
    shot_ids = jnp.arange(shots, dtype=jnp.int32)
    first_match = shot_pairs[:, 0][:, None, None] == shot_ids[None, :, None]
    second_match = shot_pairs[:, 1][:, None, None] == shot_ids[None, None, :]
    linked = jnp.any(first_match & second_match, axis=0)
    return linked | linked.T


def route_table(routes, shot_pairs):
    myself = lax.axis_index("seq")
    my_shot = myself // SHOT_DEV
    mine = lax.dynamic_slice_in_dim(routes, myself * PER_BLOCK, PER_BLOCK, 0).reshape(-1)
    shot = mine // (PER_BLOCK * SHOT_DEV)
    linked = pair_table(shot_pairs, SHOTS)
    shot_ids = jnp.arange(SHOTS, dtype=jnp.int32)
    row = jnp.any(linked & (shot_ids == my_shot)[:, None], axis=0)
    allowed = jnp.any(row[None, :] & (shot[:, None] == shot_ids[None, :]), axis=1)
    return jnp.concatenate([(shot - my_shot) % SHOTS, mine % PER_BLOCK, allowed.astype(jnp.int32)])


def fetch(table, far, buffer, sem):
    def copy(source, start, slot, at, rows):
        return pltpu.make_async_copy(
            source.at[pl.ds(start, rows), :], buffer.at[slot, pl.ds(at, rows), :], sem
        )

    def one(slot, carry):
        away = table[slot]
        group = table[FAR + slot]
        for place, offset in enumerate((1, 2, 3, 5, 6, 7)):

            @pl.when(away == offset)
            def _(place=place):
                copy(far[place], pl.multiple_of(group * GROUP, GROUP), slot, 0, GROUP).start()

        @pl.when((away == 4) & (group == 0))
        def _():
            copy(far[6], 0, slot, 0, GROUP).start()

        @pl.when((away == 4) & (group == 1))
        def _():
            copy(far[6], GROUP, slot, 0, HALF).start()
            copy(far[7], 0, slot, HALF, HALF).start()

        @pl.when((away == 4) & (group == 2))
        def _():
            copy(far[7], HALF, slot, 0, GROUP).start()

        return carry

    lax.fori_loop(0, FAR, one, 0)
    pltpu.make_async_copy(buffer, buffer, sem).wait()


def score_kernel(table, q_ref, k_ref, *rest):
    far, (w_ref, total_ref, buffer, sem) = rest[:8], rest[8:]
    fetch(table, far, buffer, sem)
    heads = q_ref.shape[1] // HD
    tokens = k_ref.shape[0]
    scale = 1.0 / HD**0.5
    lanes = lax.broadcasted_iota(jnp.int32, (GROUP, HD), 1)
    contract = (((1,), (1,)), ((), ()))
    for c in range(PER_BLOCK):
        rows = slice(c * GROUP, (c + 1) * GROUP)
        totals = jnp.zeros((GROUP, HD), jnp.float32)
        for h in range(heads):
            columns = slice(h * HD, (h + 1) * HD)
            query = q_ref[rows, columns]
            parts = [
                lax.dot_general(
                    query, k_ref[:, columns], contract, preferred_element_type=jnp.float32
                )
                * scale
            ]
            for j in range(ROUTED):
                slot = c * ROUTED + j
                score = lax.dot_general(
                    query, buffer[slot, :, columns], contract, preferred_element_type=jnp.float32
                )
                parts.append(jnp.where(table[2 * FAR + slot] == 1, score * scale, -1e30))
            scores = jnp.concatenate(parts, axis=1)
            weights = jnp.exp(scores - jnp.max(scores, axis=1, keepdims=True))
            total = jnp.sum(weights, axis=1, keepdims=True)
            totals = jnp.where(lanes == h, total, totals)
            w_ref[c * heads + h] = weights.astype(jnp.bfloat16)
        total_ref[c] = totals


def value_kernel(table, w_ref, total_ref, v_ref, *rest):
    far, (o_ref, buffer, sem) = rest[:8], rest[8:]
    fetch(table, far, buffer, sem)
    tokens, features = v_ref.shape
    heads = features // HD
    for c in range(PER_BLOCK):
        rows = slice(c * GROUP, (c + 1) * GROUP)
        for h in range(heads):
            columns = slice(h * HD, (h + 1) * HD)
            weights = w_ref[c * heads + h]
            result = jnp.dot(
                weights[:, :tokens], v_ref[:, columns], preferred_element_type=jnp.float32
            )
            for j in range(ROUTED):
                at = tokens + j * GROUP
                result += jnp.dot(
                    weights[:, at : at + GROUP],
                    buffer[c * ROUTED + j, :, columns],
                    preferred_element_type=jnp.float32,
                )
            o_ref[rows, columns] = (result / total_ref[c][:, h : h + 1]).astype(o_ref.dtype)


VMEM = pl.BlockSpec(memory_space=pltpu.VMEM)
SMEM = pl.BlockSpec(memory_space=pltpu.SMEM)
ANY = pl.BlockSpec(memory_space=pl.ANY)


def kernels(features):
    heads = features // HD
    keys = (PER_BLOCK + ROUTED) * GROUP
    scratch = [pltpu.VMEM((FAR, GROUP, features), jnp.bfloat16), pltpu.SemaphoreType.DMA]
    flops = 2 * PER_BLOCK * GROUP * keys * features
    score = pl.pallas_call(
        score_kernel,
        out_shape=(
            jax.ShapeDtypeStruct((PER_BLOCK * heads, GROUP, keys), jnp.bfloat16),
            jax.ShapeDtypeStruct((PER_BLOCK, GROUP, HD), jnp.float32),
        ),
        in_specs=[SMEM, VMEM, VMEM] + [ANY] * 8,
        out_specs=(VMEM, VMEM),
        scratch_shapes=scratch,
        compiler_params=pltpu.CompilerParams(vmem_limit_bytes=24 << 20),
        cost_estimate=pl.CostEstimate(
            flops=flops, bytes_accessed=6 << 20, transcendentals=flops // HD // 2
        ),
        name="scores",
    )
    value = pl.pallas_call(
        value_kernel,
        out_shape=jax.ShapeDtypeStruct((PER_BLOCK * GROUP, features), jnp.bfloat16),
        in_specs=[SMEM, VMEM, VMEM, VMEM] + [ANY] * 8,
        out_specs=VMEM,
        scratch_shapes=scratch,
        compiler_params=pltpu.CompilerParams(vmem_limit_bytes=24 << 20),
        cost_estimate=pl.CostEstimate(flops=flops, bytes_accessed=6 << 20, transcendentals=0),
        name="weighted_values",
    )
    return score, value


def shards(queries, keys, values, routes, shot_pairs):
    table = route_table(routes, shot_pairs)
    key_block = to_heads(keys)
    value_block = to_heads(values)
    query_block = to_heads(queries)
    score, value = kernels(key_block.shape[1])
    far_keys = ring(key_block)
    weights, totals = score(table, query_block, key_block, *far_keys)
    far_values = ring(value_block)
    return to_tokens(value(table, weights, totals, value_block, *far_values))


def solution(mesh):
    rows = P(("seq", "head"), None)
    return jax.shard_map(
        shards,
        mesh=mesh,
        in_specs=(rows, rows, rows, P(), P()),
        out_specs=rows,
        check_vma=False,
    )
```

```python
import functools

import jax
import jax.numpy as jnp
from jax import lax
from jax.experimental import pallas as pl
from jax.experimental.pallas import tpu as pltpu
from jax.sharding import PartitionSpec as P

HD = 128
GROUP = 128
SHOT_DEV = 8
ROUTED = 3
SHOTS = 8
PER_BLOCK = 3
FAR = PER_BLOCK * ROUTED
HALF = GROUP // 2


def hop(value, axis, shots):
    count = lax.axis_size(axis)
    steps = shots * SHOT_DEV
    pairs = [(source, (source + steps) % count) for source in range(count)]
    return lax.ppermute(value, axis, pairs)


def to_heads(rows):
    tokens, features = rows.shape
    parts = lax.axis_size("head")
    pieces = rows.reshape(tokens, parts, features // parts).transpose(1, 0, 2)
    got = lax.all_to_all(pieces, "head", split_axis=0, concat_axis=0, tiled=True)
    return got.reshape(parts * tokens, features // parts)


def to_tokens(block):
    parts = lax.axis_size("head")
    tokens, features = block.shape
    pieces = block.reshape(parts, tokens // parts, features)
    got = lax.all_to_all(pieces, "head", split_axis=0, concat_axis=0, tiled=True)
    return got.transpose(1, 0, 2).reshape(tokens // parts, parts * features)


def after(value, *others):
    return lax.optimization_barrier((value, *others))[0]


def in_hbm(arrays):
    return [pltpu.with_memory_space_constraint(array, pltpu.HBM) for array in arrays]


def pair_table(shot_pairs, shots):
    shot_ids = jnp.arange(shots, dtype=jnp.int32)
    first_match = shot_pairs[:, 0][:, None, None] == shot_ids[None, :, None]
    second_match = shot_pairs[:, 1][:, None, None] == shot_ids[None, None, :]
    linked = jnp.any(first_match & second_match, axis=0)
    return linked | linked.T


def route_table(routes, shot_pairs):
    myself = lax.axis_index("seq")
    my_shot = myself // SHOT_DEV
    mine = lax.dynamic_slice_in_dim(routes, myself * PER_BLOCK, PER_BLOCK, 0).reshape(-1)
    shot = mine // (PER_BLOCK * SHOT_DEV)
    linked = pair_table(shot_pairs, SHOTS)
    shot_ids = jnp.arange(SHOTS, dtype=jnp.int32)
    row = jnp.any(linked & (shot_ids == my_shot)[:, None], axis=0)
    allowed = jnp.any(row[None, :] & (shot[:, None] == shot_ids[None, :]), axis=1)
    return jnp.concatenate([(shot - my_shot) % SHOTS, mine % PER_BLOCK, allowed.astype(jnp.int32)])


def fetch(table, far, buffer, sems):
    def copy(source, start, slot, at, rows):
        pltpu.make_async_copy(
            source.at[pl.ds(start, rows), :],
            buffer.at[slot, pl.ds(at, rows), :],
            sems.at[slot // ROUTED],
        ).start()

    def one(slot, carry):
        away = table[slot]
        group = table[FAR + slot]
        for place, offset in enumerate((1, 2, 3, 5, 6, 7)):

            @pl.when(away == offset)
            def _(place=place):
                copy(far[place], pl.multiple_of(group * GROUP, GROUP), slot, 0, GROUP)

        @pl.when((away == 4) & (group == 0))
        def _():
            copy(far[6], 0, slot, 0, GROUP)

        @pl.when((away == 4) & (group == 1))
        def _():
            copy(far[6], GROUP, slot, 0, HALF)
            copy(far[7], 0, slot, HALF, HALF)

        @pl.when((away == 4) & (group == 2))
        def _():
            copy(far[7], HALF, slot, 0, GROUP)

        return carry

    lax.fori_loop(0, FAR, one, 0)


def arrived(buffer, sems, c):
    slots = buffer.at[pl.ds(c * ROUTED, ROUTED)]
    pltpu.make_async_copy(slots, slots, sems.at[c]).wait()


def score_kernel(table, q_ref, k_ref, *rest):
    far, (w_ref, total_ref, buffer, sems) = rest[:8], rest[8:]
    fetch(table, far, buffer, sems)
    heads = q_ref.shape[1] // HD
    tokens = k_ref.shape[0]
    scale = 1.0 / HD**0.5
    lanes = lax.broadcasted_iota(jnp.int32, (GROUP, HD), 1)
    contract = (((1,), (1,)), ((), ()))
    for c in range(PER_BLOCK):
        arrived(buffer, sems, c)
        rows = slice(c * GROUP, (c + 1) * GROUP)
        totals = jnp.zeros((GROUP, HD), jnp.float32)
        for h in range(heads):
            columns = slice(h * HD, (h + 1) * HD)
            query = q_ref[rows, columns]
            parts = [
                lax.dot_general(
                    query, k_ref[:, columns], contract, preferred_element_type=jnp.float32
                )
                * scale
            ]
            for j in range(ROUTED):
                slot = c * ROUTED + j
                score = lax.dot_general(
                    query, buffer[slot, :, columns], contract, preferred_element_type=jnp.float32
                )
                parts.append(jnp.where(table[2 * FAR + slot] == 1, score * scale, -1e30))
            scores = jnp.concatenate(parts, axis=1)
            weights = jnp.exp(scores - jnp.max(scores, axis=1, keepdims=True))
            total = jnp.sum(weights, axis=1, keepdims=True)
            totals = jnp.where(lanes == h, total, totals)
            w_ref[c * heads + h] = weights.astype(jnp.bfloat16)
        total_ref[c] = totals


def value_kernel(table, w_ref, total_ref, v_ref, *rest):
    far, (o_ref, buffer, sems) = rest[:8], rest[8:]
    fetch(table, far, buffer, sems)
    tokens, features = v_ref.shape
    heads = features // HD
    for c in range(PER_BLOCK):
        arrived(buffer, sems, c)
        rows = slice(c * GROUP, (c + 1) * GROUP)
        for h in range(heads):
            columns = slice(h * HD, (h + 1) * HD)
            weights = w_ref[c * heads + h]
            result = jnp.dot(
                weights[:, :tokens], v_ref[:, columns], preferred_element_type=jnp.float32
            )
            for j in range(ROUTED):
                at = tokens + j * GROUP
                result += jnp.dot(
                    weights[:, at : at + GROUP],
                    buffer[c * ROUTED + j, :, columns],
                    preferred_element_type=jnp.float32,
                )
            o_ref[rows, columns] = (result / total_ref[c][:, h : h + 1]).astype(o_ref.dtype)


VMEM = pl.BlockSpec(memory_space=pltpu.VMEM)
SMEM = pl.BlockSpec(memory_space=pltpu.SMEM)
ANY = pl.BlockSpec(memory_space=pl.ANY)


def kernels(features):
    heads = features // HD
    keys = (PER_BLOCK + ROUTED) * GROUP
    scratch = [pltpu.VMEM((FAR, GROUP, features), jnp.bfloat16), pltpu.SemaphoreType.DMA((PER_BLOCK,))]
    flops = 2 * PER_BLOCK * GROUP * keys * features
    score = pl.pallas_call(
        score_kernel,
        out_shape=(
            jax.ShapeDtypeStruct((PER_BLOCK * heads, GROUP, keys), jnp.bfloat16),
            jax.ShapeDtypeStruct((PER_BLOCK, GROUP, HD), jnp.float32),
        ),
        in_specs=[SMEM, VMEM, VMEM] + [ANY] * 8,
        out_specs=(VMEM, VMEM),
        scratch_shapes=scratch,
        compiler_params=pltpu.CompilerParams(vmem_limit_bytes=24 << 20),
        cost_estimate=pl.CostEstimate(
            flops=flops, bytes_accessed=6 << 20, transcendentals=flops // HD // 2
        ),
        name="scores",
    )
    value = pl.pallas_call(
        value_kernel,
        out_shape=jax.ShapeDtypeStruct((PER_BLOCK * GROUP, features), jnp.bfloat16),
        in_specs=[SMEM, VMEM, VMEM, VMEM] + [ANY] * 8,
        out_specs=VMEM,
        scratch_shapes=scratch,
        compiler_params=pltpu.CompilerParams(vmem_limit_bytes=24 << 20),
        cost_estimate=pl.CostEstimate(flops=flops, bytes_accessed=6 << 20, transcendentals=0),
        name="weighted_values",
    )
    return score, value


def shards(queries, keys, values, routes, shot_pairs):
    table = route_table(routes, shot_pairs)
    up = functools.partial(hop, axis="seq", shots=1)
    down = functools.partial(hop, axis="seq", shots=-1)
    key_block = to_heads(keys)
    value_block = to_heads(values)
    query_block = to_heads(queries)
    k_up1, k_down1 = up(key_block), down(key_block)
    v_up1, v_down1 = up(value_block), down(value_block)
    k_up2, k_down2 = up(k_up1), down(k_down1)
    v_up2, v_down2 = up(v_up1), down(v_down1)
    k_up3, k_down3 = up(k_up2), down(k_down2)
    v_up3, v_down3 = up(v_up2), down(v_down2)
    middle = key_block.shape[0] // 2
    k_upper, k_lower = up(k_up3[:middle]), down(k_down3[middle:])
    v_upper, v_lower = up(v_up3[:middle]), down(v_down3[middle:])
    score, value = kernels(key_block.shape[1])
    far_keys = (k_down1, k_down2, k_down3, k_up3, k_up2, k_up1, k_upper, k_lower)
    far_values = (v_down1, v_down2, v_down3, v_up3, v_up2, v_up1, v_upper, v_lower)
    far_keys, far_values = in_hbm(far_keys), in_hbm(far_values)
    weights, totals = score(table, query_block, key_block, *far_keys)
    return to_tokens(value(table, weights, totals, value_block, *far_values))


def solution(mesh):
    rows = P(("seq", "head"), None)
    return jax.shard_map(
        shards,
        mesh=mesh,
        in_specs=(rows, rows, rows, P(), P()),
        out_specs=rows,
        check_vma=False,
    )
```

```python
import functools

import jax
import jax.numpy as jnp
from jax import lax
from jax.experimental import pallas as pl
from jax.experimental.pallas import tpu as pltpu
from jax.sharding import PartitionSpec as P

HD = 128
GROUP = 128
SHOT_DEV = 8
ROUTED = 3
SHOTS = 8
PER_BLOCK = 3
FAR = PER_BLOCK * ROUTED


def hop(value, axis, shots):
    count = lax.axis_size(axis)
    steps = shots * SHOT_DEV
    pairs = [(source, (source + steps) % count) for source in range(count)]
    return lax.ppermute(value, axis, pairs)


def to_heads(rows):
    tokens, features = rows.shape
    parts = lax.axis_size("head")
    pieces = rows.reshape(tokens, parts, features // parts).transpose(1, 0, 2)
    got = lax.all_to_all(pieces, "head", split_axis=0, concat_axis=0, tiled=True)
    return got.reshape(parts * tokens, features // parts)


def to_tokens(block):
    parts = lax.axis_size("head")
    tokens, features = block.shape
    pieces = block.reshape(parts, tokens // parts, features)
    got = lax.all_to_all(pieces, "head", split_axis=0, concat_axis=0, tiled=True)
    return got.transpose(1, 0, 2).reshape(tokens // parts, parts * features)


def after(value, *others):
    return lax.optimization_barrier((value, *others))[0]


def in_hbm(arrays):
    return [pltpu.with_memory_space_constraint(array, pltpu.HBM) for array in arrays]


def pair_table(shot_pairs, shots):
    shot_ids = jnp.arange(shots, dtype=jnp.int32)
    first_match = shot_pairs[:, 0][:, None, None] == shot_ids[None, :, None]
    second_match = shot_pairs[:, 1][:, None, None] == shot_ids[None, None, :]
    linked = jnp.any(first_match & second_match, axis=0)
    return linked | linked.T


def route_table(routes, shot_pairs):
    myself = lax.axis_index("seq")
    my_shot = myself // SHOT_DEV
    mine = lax.dynamic_slice_in_dim(routes, myself * PER_BLOCK, PER_BLOCK, 0).reshape(-1)
    shot = mine // (PER_BLOCK * SHOT_DEV)
    linked = pair_table(shot_pairs, SHOTS)
    shot_ids = jnp.arange(SHOTS, dtype=jnp.int32)
    row = jnp.any(linked & (shot_ids == my_shot)[:, None], axis=0)
    allowed = jnp.any(row[None, :] & (shot[:, None] == shot_ids[None, :]), axis=1)
    return jnp.concatenate([(shot - my_shot) % SHOTS, mine % PER_BLOCK, allowed.astype(jnp.int32)])


def fetch(table, far, buffer, sems):
    def copy(source, start, slot, at, rows):
        pltpu.make_async_copy(
            source.at[pl.ds(start, rows), :],
            buffer.at[slot, pl.ds(at, rows), :],
            sems.at[slot // ROUTED],
        ).start()

    def one(slot, carry):
        away = table[slot]
        group = table[FAR + slot]
        for place, offset in enumerate((1, 2, 3, 5, 6, 7)):

            @pl.when(away == offset)
            def _(place=place):
                copy(far[place], pl.multiple_of(group * GROUP, GROUP), slot, 0, GROUP)

        split = far[6].shape[0]
        for g in range(PER_BLOCK):

            @pl.when((away == 4) & (group == g))
            def _(g=g):
                first = g * GROUP
                cut = min(max(split - first, 0), GROUP)
                if cut > 0:
                    copy(far[6], first, slot, 0, cut)
                if cut < GROUP:
                    copy(far[7], first + cut - split, slot, cut, GROUP - cut)

        return carry

    lax.fori_loop(0, FAR, one, 0)


def arrived(buffer, sems, c):
    slots = buffer.at[pl.ds(c * ROUTED, ROUTED)]
    pltpu.make_async_copy(slots, slots, sems.at[c]).wait()


def score_kernel(table, q_ref, k_ref, *rest):
    far, (near_ref, far_ref, total_ref, buffer, sems) = rest[:8], rest[8:]
    fetch(table, far, buffer, sems)
    heads = q_ref.shape[1] // HD
    tokens = k_ref.shape[0]
    scale = 1.0 / HD**0.5
    lanes = lax.broadcasted_iota(jnp.int32, (GROUP, HD), 1)
    contract = (((1,), (1,)), ((), ()))
    for c in range(PER_BLOCK):
        arrived(buffer, sems, c)
        rows = slice(c * GROUP, (c + 1) * GROUP)
        totals = jnp.zeros((GROUP, HD), jnp.float32)
        for h in range(heads):
            columns = slice(h * HD, (h + 1) * HD)
            query = q_ref[rows, columns]
            parts = [
                lax.dot_general(
                    query, k_ref[:, columns], contract, preferred_element_type=jnp.float32
                )
                * scale
            ]
            for j in range(ROUTED):
                slot = c * ROUTED + j
                score = lax.dot_general(
                    query, buffer[slot, :, columns], contract, preferred_element_type=jnp.float32
                )
                parts.append(jnp.where(table[2 * FAR + slot] == 1, score * scale, -1e30))
            scores = jnp.concatenate(parts, axis=1)
            weights = jnp.exp(scores - jnp.max(scores, axis=1, keepdims=True))
            total = jnp.sum(weights, axis=1, keepdims=True)
            totals = jnp.where(lanes == h, total, totals)
            weights = weights.astype(jnp.bfloat16)
            near_ref[h, rows, :] = weights[:, :tokens]
            far_ref[c * heads + h] = weights[:, tokens:]
        total_ref[c] = totals


def value_kernel(table, near_ref, far_ref, total_ref, v_ref, *rest):
    far, (o_ref, buffer, partial, sems) = rest[:8], rest[8:]
    fetch(table, far, buffer, sems)
    tokens, features = v_ref.shape
    heads = features // HD
    for h in range(heads):
        columns = slice(h * HD, (h + 1) * HD)
        partial[:, columns] = jnp.dot(
            near_ref[h], v_ref[:, columns], preferred_element_type=jnp.float32
        )
    for c in range(PER_BLOCK):
        arrived(buffer, sems, c)
        rows = slice(c * GROUP, (c + 1) * GROUP)
        slots = slice(c * ROUTED, (c + 1) * ROUTED)
        for h in range(heads):
            columns = slice(h * HD, (h + 1) * HD)
            far_values = buffer[slots, :, columns].reshape(ROUTED * GROUP, HD)
            result = partial[rows, columns] + jnp.dot(
                far_ref[c * heads + h], far_values, preferred_element_type=jnp.float32
            )
            o_ref[rows, columns] = (result / total_ref[c][:, h : h + 1]).astype(o_ref.dtype)


VMEM = pl.BlockSpec(memory_space=pltpu.VMEM)
SMEM = pl.BlockSpec(memory_space=pltpu.SMEM)
ANY = pl.BlockSpec(memory_space=pl.ANY)


def kernels(features):
    heads = features // HD
    keys = (PER_BLOCK + ROUTED) * GROUP
    scratch = [pltpu.VMEM((FAR, GROUP, features), jnp.bfloat16), pltpu.SemaphoreType.DMA((PER_BLOCK,))]
    flops = 2 * PER_BLOCK * GROUP * keys * features
    score = pl.pallas_call(
        score_kernel,
        out_shape=(
            jax.ShapeDtypeStruct((heads, PER_BLOCK * GROUP, PER_BLOCK * GROUP), jnp.bfloat16),
            jax.ShapeDtypeStruct((PER_BLOCK * heads, GROUP, ROUTED * GROUP), jnp.bfloat16),
            jax.ShapeDtypeStruct((PER_BLOCK, GROUP, HD), jnp.float32),
        ),
        in_specs=[SMEM, VMEM, VMEM] + [ANY] * 8,
        out_specs=(VMEM, VMEM, VMEM),
        scratch_shapes=scratch,
        compiler_params=pltpu.CompilerParams(vmem_limit_bytes=24 << 20),
        cost_estimate=pl.CostEstimate(
            flops=flops, bytes_accessed=6 << 20, transcendentals=flops // HD // 2
        ),
        name="scores",
    )
    value = pl.pallas_call(
        value_kernel,
        out_shape=jax.ShapeDtypeStruct((PER_BLOCK * GROUP, features), jnp.bfloat16),
        in_specs=[SMEM, VMEM, VMEM, VMEM, VMEM] + [ANY] * 8,
        out_specs=VMEM,
        scratch_shapes=[
            scratch[0],
            pltpu.VMEM((PER_BLOCK * GROUP, features), jnp.float32),
            scratch[1],
        ],
        compiler_params=pltpu.CompilerParams(vmem_limit_bytes=24 << 20),
        cost_estimate=pl.CostEstimate(flops=flops, bytes_accessed=6 << 20, transcendentals=0),
        name="weighted_values",
    )
    return score, value


def shards(queries, keys, values, routes, shot_pairs):
    table = route_table(routes, shot_pairs)
    up = functools.partial(hop, axis="seq", shots=1)
    down = functools.partial(hop, axis="seq", shots=-1)
    key_block = to_heads(keys)
    value_block = to_heads(values)
    query_block = to_heads(queries)
    k_up1, k_down1 = up(key_block), down(key_block)
    v_up1, v_down1 = up(value_block), down(value_block)
    k_up2, k_down2 = up(k_up1), down(k_down1)
    v_up2, v_down2 = up(v_up1), down(v_down1)
    k_up3, k_down3 = up(k_up2), down(k_down2)
    v_up3, v_down3 = up(v_up2), down(v_down2)
    middle = key_block.shape[0] // 2
    k_upper, k_lower = up(k_up3[:middle]), down(k_down3[middle:])
    more = middle + GROUP // 4
    v_upper, v_lower = up(v_up3[:more]), down(v_down3[more:])
    score, value = kernels(key_block.shape[1])
    far_keys = (k_down1, k_down2, k_down3, k_up3, k_up2, k_up1, k_upper, k_lower)
    far_values = (v_down1, v_down2, v_down3, v_up3, v_up2, v_up1, v_upper, v_lower)
    far_keys, far_values = in_hbm(far_keys), in_hbm(far_values)
    near, routed, totals = score(table, query_block, key_block, *far_keys)
    return to_tokens(value(table, near, routed, totals, value_block, *far_values))


def solution(mesh):
    rows = P(("seq", "head"), None)
    return jax.shard_map(
        shards,
        mesh=mesh,
        in_specs=(rows, rows, rows, P(), P()),
        out_specs=rows,
        check_vma=False,
    )
```
